256 devices in a mesh: inst: 32 (over x, y, core), tp: 8 (over z).
Axes of the slice: x: 4, y: 4, z: 8, core: 2. Of those that a mesh axis runs over, the one named last changes fastest.
Arguments:
- queries: bfloat16 [32, 4, 8192], P('inst', None, 'tp'), may hold values from -240 to 240
- new_keys: bfloat16 [32, 4, 1024], P('inst', None, 'tp'), may hold values from -6 to 6
- new_values: bfloat16 [32, 4, 1024], P('inst', None, 'tp'), may hold values from -6 to 6
- key_blocks: bfloat16 [256, 2048, 1024], P('inst', None, 'tp'), may hold values from -6 to 6
- value_blocks: bfloat16 [256, 2048, 1024], P('inst', None, 'tp'), may hold values from -6 to 6
- slot_rows: int32 [256], P('inst'), may hold values from 0 to 31
- slot_blocks: int32 [256], P('inst'), may hold values from 0 to 64, as said below
- lengths: int32 [32], replicated, may hold values from 1 to 131072, as said below
- out_weight: bfloat16 [8192, 8192], P('tp', 'inst'), may hold values from -0.0625 to 0.0625
Outputs:
- layer_out: bfloat16 [32, 4, 8192], P('tp', None, 'inst')
The draws below stay inside these ranges and needn't reach their ends.
Inputs may be any that keep to these rules, and one draw needn't show every extreme that they name: Every block b < ceil(lengths[r] / 2048) of sequence r sits in exactly one slot, with slot_rows = r and slot_blocks = b; every other slot has slot_blocks = 64. The blocks of every sequence but the longest sit in the slots of inst device r; the longest sequence's blocks fill the slots left free on any device. `lengths`: one sequence holds exactly 131072 tokens; every other holds at most 12288.
All inputs are finite; a program needn't handle non-finite values.
Results may differ from the reference program's by a relative error of at most 0.0057.
Values may be sent and summed in bfloat16 or wider, within the bound.
No kernel may reach another device: no remote copies, remote signals or barrier semaphores. Data moves between devices by JAX's collectives and lax.ppermute only.
A program may use at most 64 MiB of HBM per device.

```python
import jax
import jax.numpy as jnp
from jax import lax

D = 8192
KVH = 8
HQ = 8
HD = 128
BLK = 2048
STEPS = 4
SLOTS = 8
ROWS = 32
MOST = 64
LOWMAX = 6
N_INST = 32


def layout(key):
    capacity = N_INST * SLOTS
    key_count, key_long, key_tail, key_perm, key_fill = jax.random.split(key, 5)
    row_ids = jnp.arange(ROWS, dtype=jnp.int32)
    counts = jax.random.randint(key_count, (ROWS,), 1, LOWMAX + 1)
    longest = jax.random.randint(key_long, (), 0, ROWS)
    counts = jnp.where(row_ids == longest, MOST, counts).astype(jnp.int32)
    tails = jax.random.randint(key_tail, (ROWS,), 1, BLK + 1)
    tails = jnp.where(row_ids == longest, BLK, tails)
    lengths = ((counts - 1) * BLK + tails).astype(jnp.int32)
    entries = jnp.arange(capacity, dtype=jnp.int32)
    device = entries // SLOTS
    local = entries % SLOTS
    home_used = (device != longest) & (local < counts[device])
    free = jnp.logical_not(home_used)
    free_rank = (jnp.cumsum(free.astype(jnp.int32)) - 1).astype(jnp.int32)
    lent_used = free & (free_rank < MOST)
    filler = jax.random.randint(key_fill, (capacity,), 0, ROWS)
    owner = jnp.where(home_used, device, jnp.where(lent_used, longest, filler)).astype(jnp.int32)
    block_id = jnp.where(home_used, local, jnp.where(lent_used, free_rank, MOST)).astype(jnp.int32)
    device_keys = jax.random.split(key_perm, N_INST)
    within = jax.vmap(lambda k: jax.random.permutation(k, SLOTS))(device_keys).astype(jnp.int32)
    order = (jnp.arange(N_INST, dtype=jnp.int32)[:, None] * SLOTS + within).reshape(capacity)
    return (owner[order], block_id[order], lengths)


def draw_slot_rows(key, part):
    return layout(key)[0]


def draw_slot_blocks(key, part):
    return layout(key)[1]


def draw_lengths(key, part):
    return layout(key)[2]


def draw_queries(key, part):
    key = jax.random.fold_in(key, 7)
    base = jnp.clip(jax.random.normal(key, (ROWS, STEPS, KVH * HQ * HD), jnp.float32), -6.0, 6.0)
    return base.astype(jnp.bfloat16)


def steps_of(key, shape, shards, smallest, largest):
    factor_of, own = 1.0, jax.random.fold_in(key, 6)
    for dim, blocks in shards:
        steps = jnp.exp(jax.random.uniform(jax.random.fold_in(own, dim), (blocks,), jnp.float32, smallest / len(shards), largest / len(shards)))
        factor_of = factor_of * jnp.repeat(steps, shape[dim] // blocks).reshape([-1 if axis == dim else 1 for axis in range(len(shape))])
    return factor_of


def noise(rng, extent, deviation, most, cuts=(), kind=jnp.bfloat16):
    level = steps_of(rng, extent, cuts, -0.22, 0.18) if cuts else 1.0
    values = jax.random.normal(rng, extent, jnp.float32) * deviation * level
    return jnp.minimum(jnp.maximum(values, -most), most).astype(kind)


def setup_inputs(seed: int = 0) -> dict:
    streams_of = jax.random.split(jax.random.key(seed), 10)
    return {
        "queries": draw_queries(jax.random.fold_in(streams_of[9], 71), 0),
        "new_keys": noise(streams_of[1], (ROWS, STEPS, KVH * HD), 1.0, 6.0, ((0, 32), (2, 8))),
        "new_values": noise(streams_of[2], (ROWS, STEPS, KVH * HD), 1.0, 6.0, ((0, 32), (2, 8))),
        "key_blocks": noise(streams_of[3], (N_INST * SLOTS, BLK, KVH * HD), 1.0, 6.0, ((0, 32), (2, 8))),
        "value_blocks": noise(streams_of[4], (N_INST * SLOTS, BLK, KVH * HD), 1.0, 6.0, ((0, 32), (2, 8))),
        "slot_rows": draw_slot_rows(jax.random.fold_in(streams_of[9], 71), 0),
        "slot_blocks": draw_slot_blocks(jax.random.fold_in(streams_of[9], 71), 0),
        "lengths": draw_lengths(jax.random.fold_in(streams_of[9], 71), 0),
        "out_weight": noise(streams_of[8], (KVH * HQ * HD, D), (KVH * HQ * HD) ** -0.5, 0.0625, ((0, 8), (1, 32))),
    }


NEG = -1e30


def reference(queries, new_keys, new_values, key_blocks, value_blocks, slot_rows, slot_blocks, lengths, out_weight):
    scale = HD ** -0.5
    query_all = queries.reshape(ROWS, STEPS, KVH, HQ, HD).astype(jnp.float32)

    def one_slot(items):
        keys, vals, owner, block_id = items
        query_row = query_all[owner]
        keys_f = keys.reshape(BLK, KVH, HD).astype(jnp.float32)
        vals_f = vals.reshape(BLK, KVH, HD).astype(jnp.float32)
        scores = jnp.einsum('tghd,bgd->tghb', query_row, keys_f) * scale
        position = block_id * BLK + jnp.arange(BLK, dtype=jnp.int32)
        valid = position < lengths[owner]
        scores = jnp.where(valid, scores, NEG)
        part_max = jnp.max(scores, axis=-1)
        weights = jnp.where(valid, jnp.exp(scores - part_max[..., None]), 0.0)
        part_sum = jnp.sum(weights, axis=-1)
        rounded = weights.astype(jnp.bfloat16).astype(jnp.float32)
        part_acc = jnp.einsum('tghb,bgd->tghd', rounded, vals_f)
        return part_max, part_sum, part_acc

    slot_max, slot_sum, slot_acc = lax.map(one_slot, (key_blocks, value_blocks, slot_rows, slot_blocks))

    fresh_keys = new_keys.reshape(ROWS, STEPS, KVH, HD).astype(jnp.float32)
    fresh_vals = new_values.reshape(ROWS, STEPS, KVH, HD).astype(jnp.float32)
    own_scores = jnp.einsum('rtghd,rugd->rtghu', query_all, fresh_keys) * scale
    causal = jnp.arange(STEPS)[:, None] >= jnp.arange(STEPS)[None, :]
    causal = causal[None, :, None, None, :]
    own_scores = jnp.where(causal, own_scores, NEG)
    own_max = jnp.max(own_scores, axis=-1)
    own_weights = jnp.where(causal, jnp.exp(own_scores - own_max[..., None]), 0.0)
    own_sum = jnp.sum(own_weights, axis=-1)
    own_acc = jnp.einsum('rtghu,rugd->rtghd', own_weights.astype(jnp.bfloat16).astype(jnp.float32), fresh_vals)

    onehot = slot_rows[:, None] == jnp.arange(ROWS, dtype=jnp.int32)[None, :]
    masked_max = jnp.where(onehot[:, :, None, None, None], slot_max[:, None], NEG)
    top = jnp.maximum(jnp.max(masked_max, axis=0), own_max)
    slot_factor = jnp.exp(slot_max - top[slot_rows])
    own_factor = jnp.exp(own_max - top)
    onehot_f = onehot.astype(jnp.float32)
    total = own_sum * own_factor + jnp.einsum('sr,stgh->rtgh', onehot_f, slot_sum * slot_factor, precision=lax.Precision.HIGHEST)
    weighted = own_acc * own_factor[..., None] + jnp.einsum('sr,stghd->rtghd', onehot_f, slot_acc * slot_factor[..., None], precision=lax.Precision.HIGHEST)
    attended = (weighted / total[..., None]).astype(jnp.bfloat16).reshape(ROWS * STEPS, KVH * HQ * HD)
    projected = jnp.dot(attended, out_weight, preferred_element_type=jnp.float32)
    return projected.reshape(ROWS, STEPS, D).astype(jnp.bfloat16)
```

```python
import functools
import math

import jax
import jax.numpy as jnp
from jax import lax
from jax.experimental import pallas as pl
from jax.experimental.pallas import tpu as pltpu
from jax.sharding import PartitionSpec as P

HQ = 8
HD = 128
WIDTH = HQ * HD
NEG = -1e30
FLOOR = -1e29
C = HD ** (-0.5) / math.log(2.0)
PIECES = 3
CORES = 2


def longest_row(lengths_ref):
    row, most = jnp.int32(0), lengths_ref[0]
    for r in range(1, lengths_ref.shape[0]):
        here = lengths_ref[r]
        row = jnp.where(here > most, r, row)
        most = jnp.maximum(here, most)
    return row


def pieces_of(x):
    parts = []
    for _ in range(PIECES):
        part = x.astype(jnp.bfloat16).astype(jnp.float32)
        parts.append(part)
        x = x - part
    return parts


def rows_of_heads(q):
    return jnp.concatenate([q[:, h * HD : (h + 1) * HD] for h in range(HQ)], axis=0)


def spread_kernel(
    block_len,
    me_ref,
    rows_hbm,
    blocks_hbm,
    lengths_hbm,
    query_hbm,
    new_key_hbm,
    new_value_hbm,
    other_ref,
    spread_ref,
    query_ref,
    new_key_ref,
    new_value_ref,
    plan_ref,
    rows_ref,
    blocks_ref,
    lengths_ref,
    sems,
):
    slots = rows_ref.shape[0]
    copies = [
        pltpu.make_async_copy(source, target, sems.at[k])
        for k, (source, target) in enumerate(
            [
                (lengths_hbm, lengths_ref),
                (query_hbm.at[0], query_ref),
                (rows_hbm, rows_ref),
                (blocks_hbm, blocks_ref),
                (new_key_hbm.at[0], new_key_ref),
                (new_value_hbm.at[0], new_value_ref),
            ]
        )
    ]
    for copy in copies:
        copy.start()
    for copy in copies:
        copy.wait()
    me = me_ref[0]
    longest = longest_row(lengths_ref)
    asked = jnp.where(
        me // CORES * CORES + (CORES - 1 - me % CORES) == longest,
        other_ref[0].astype(jnp.float32),
        query_ref[...].astype(jnp.float32),
    ).astype(jnp.bfloat16)
    spread_ref[...] = jnp.broadcast_to(asked[None], spread_ref.shape)
    plan_ref[0] = longest
    plan_ref[1] = me
    for s in range(slots):
        row = rows_ref[s]
        in_long = row == longest
        valid = jnp.clip(lengths_ref[row] - blocks_ref[s] * block_len, 0, block_len)
        plan_ref[2 + s] = in_long.astype(jnp.int32)
        plan_ref[2 + slots + s] = jnp.where(in_long | (row == me), valid, 0)


def attend_kernel(
    plan_ref,
    asked_ref,
    query_ref,
    new_key_ref,
    new_value_ref,
    key_ref,
    value_ref,
    out_ref,
    queries,
    scores,
):
    slots, block_len, _ = key_ref.shape
    steps = query_ref.shape[0]
    heads = HQ * steps
    longest = plan_ref[0]
    mine = plan_ref[1] == longest
    own_query = rows_of_heads(query_ref[...].astype(jnp.float32))
    queries[0] = own_query.astype(jnp.bfloat16)
    queries[1] = rows_of_heads(asked_ref[longest // CORES].astype(jnp.float32)).astype(jnp.bfloat16)

    column = lax.broadcasted_iota(jnp.int32, (heads, block_len), 1)
    tops = []
    for s in range(slots):
        score = lax.dot_general(
            queries[plan_ref[2 + s]],
            key_ref[s],
            (((1,), (1,)), ((), ())),
            preferred_element_type=jnp.float32,
        )
        score = jnp.where(column < plan_ref[2 + slots + s], score, NEG)
        scores[s] = score
        tops.append(jnp.maximum(jnp.max(score, axis=1, keepdims=True), FLOOR))

    step_of = lax.broadcasted_iota(jnp.int32, (heads, 1), 0) % steps
    fresh = []
    for u in range(steps):
        score = jnp.sum(
            own_query * new_key_ref[u : u + 1, :].astype(jnp.float32), axis=1, keepdims=True
        )
        fresh.append(jnp.where(step_of >= u, score, NEG))
    top = functools.reduce(jnp.maximum, fresh)
    total = jnp.zeros_like(top)
    acc = jnp.zeros((heads, HD), jnp.float32)
    for u in range(steps):
        weight = jnp.exp2((fresh[u] - top) * C)
        total += weight
        acc += weight.astype(jnp.bfloat16).astype(jnp.float32) * new_value_ref[
            u : u + 1, :
        ].astype(jnp.float32)
    parts = [(mine, top, total, acc)]

    for s in range(slots):
        weights = jnp.exp2((scores[s] - tops[s]) * C)
        total = jnp.sum(weights, axis=1, keepdims=True)
        acc = jnp.dot(
            weights.astype(jnp.bfloat16), value_ref[s], preferred_element_type=jnp.float32
        )
        parts.append((plan_ref[2 + s] == 1, tops[s], total, acc))

    merged = []
    for wanted in (False, True):
        best = functools.reduce(
            jnp.maximum, [jnp.where(in_long == wanted, top, FLOOR) for in_long, top, _, _ in parts]
        )
        sum_all = jnp.zeros_like(best)
        acc_all = jnp.zeros((heads, HD), jnp.float32)
        for in_long, top, total, acc in parts:
            factor = jnp.where(in_long == wanted, jnp.exp2(jnp.minimum(top - best, 0.0) * C), 0.0)
            sum_all += factor * total
            acc_all += factor * acc
        merged.append((best, sum_all, acc_all))

    _, own_sum, own_acc = merged[0]
    attended = own_acc / jnp.where(own_sum > 0.0, own_sum, 1.0)
    long_top, long_sum, long_acc = merged[1]
    stats = pieces_of(long_top) + pieces_of(long_sum)
    lane = lax.broadcasted_iota(jnp.int32, (steps, HD), 1)
    packed = jnp.zeros((steps, HD), jnp.float32)
    for h in range(HQ):
        rows = slice(h * steps, (h + 1) * steps)
        for k, piece in enumerate(stats):
            packed = jnp.where(lane == k * HQ + h, piece[rows], packed)
    heads_of = lambda x: [x[h * steps : (h + 1) * steps] for h in range(HQ)]
    sent = jnp.concatenate(heads_of(attended) + heads_of(long_acc) + [packed], axis=1)
    out_ref[...] = sent.astype(jnp.bfloat16)


def project_kernel(steps, plan_ref, mine_ref, other_ref, weight_ref, out_ref):
    half, _ = mine_ref.shape
    rows = CORES * half
    longest = plan_ref[0]
    first = plan_ref[1] % CORES == 0
    both = lambda cols: jnp.concatenate([mine_ref[:, cols], other_ref[:, cols]], axis=0)
    stats = both(slice(2 * WIDTH, 2 * WIDTH + HD))
    lane = lax.broadcasted_iota(jnp.int32, (HD, WIDTH), 0)
    chosen = lane % HQ == lax.broadcasted_iota(jnp.int32, (HD, WIDTH), 1) // HD
    split = PIECES * HQ
    pick_top = jnp.where(chosen & (lane < split), 1.0, 0.0).astype(jnp.bfloat16)
    pick_sum = jnp.where(chosen & (lane >= split), 1.0, 0.0).astype(jnp.bfloat16)
    tops = jnp.dot(stats, pick_top, preferred_element_type=jnp.float32)
    sums = jnp.dot(stats, pick_sum, preferred_element_type=jnp.float32)
    accs = both(slice(WIDTH, 2 * WIDTH)).astype(jnp.float32)

    pair = 2 * steps
    fold = lambda x: x.reshape(-1, pair, x.shape[-1])
    best = jnp.max(fold(tops), axis=0)
    best = jnp.maximum(best, pltpu.roll(best, steps, 0))
    factor = jnp.exp2((fold(tops) - best[None]) * C)
    total = jnp.sum(factor * fold(sums), axis=0)
    weighted = jnp.sum(factor * fold(accs), axis=0)
    total = total + pltpu.roll(total, steps, 0)
    weighted = weighted + pltpu.roll(weighted, steps, 0)
    merged = weighted / total

    own = mine_ref[:, :WIDTH].astype(jnp.float32)
    other = other_ref[:, :WIDTH].astype(jnp.float32)
    own, other = jnp.where(first, own, other), jnp.where(first, other, own)
    shape = (half // pair, pair, WIDTH)
    chip = lax.broadcasted_iota(jnp.int32, shape, 0) * (pair // steps)
    chip = chip + lax.broadcasted_iota(jnp.int32, shape, 1) // steps
    attended = [
        jnp.where(chip * CORES + core == longest, merged[None], fold(part)).reshape(half, WIDTH)
        for core, part in enumerate((own, other))
    ]
    product = jnp.dot(
        jnp.concatenate(attended, axis=0).astype(jnp.bfloat16),
        weight_ref[...],
        preferred_element_type=jnp.float32,
    )
    shares, each, cols = out_ref.shape
    product = product.reshape(CORES, shares, each // CORES, cols)
    out_ref[...] = jnp.concatenate([product[c] for c in range(CORES)], axis=1).astype(out_ref.dtype)


def add_kernel(shares_ref, out_ref):
    rows, steps, _ = out_ref.shape
    summed = jnp.sum(shares_ref[...].astype(jnp.float32), axis=0)
    for core in range(CORES):
        for k in range(rows // CORES):
            at = (core * (rows // CORES) + k) * steps
            out_ref[k * CORES + core] = summed[at : at + steps].astype(out_ref.dtype)


SMEM = pl.BlockSpec(memory_space=pltpu.SMEM)
VMEM = pl.BlockSpec(memory_space=pltpu.VMEM)
HBM = pl.BlockSpec(memory_space=pltpu.HBM)


def near(x):
    return pltpu.with_memory_space_constraint(x, pltpu.VMEM)


def far(x):
    return pltpu.with_memory_space_constraint(x, pltpu.HBM)


def body(
    queries,
    new_keys,
    new_values,
    key_blocks,
    value_blocks,
    slot_rows,
    slot_blocks,
    lengths,
    out_weight,
):
    _, steps, width = queries.shape
    slots, block_len, _ = key_blocks.shape
    heads = HQ * steps
    devices = lax.axis_size("inst")
    chips = devices // CORES
    shares = lax.axis_size("tp")
    me = lax.axis_index("inst").astype(jnp.int32).reshape(1)
    same_core = [[chip * CORES + core for chip in range(chips)] for core in range(CORES)]
    core_pairs = [(i, i ^ 1) for i in range(devices)]
    params = pltpu.CompilerParams(vmem_limit_bytes=24 * 1024 * 1024)

    def over_chips(x):
        return lax.all_to_all(x, "inst", 0, 0, tiled=True, axis_index_groups=same_core)

    spread, query, new_key, new_value, plan = pl.pallas_call(
        functools.partial(spread_kernel, block_len),
        out_shape=[
            pltpu.VMEM((chips, steps, width), jnp.bfloat16),
            pltpu.VMEM((steps, width), jnp.bfloat16),
            pltpu.VMEM((steps, HD), jnp.bfloat16),
            pltpu.VMEM((steps, HD), jnp.bfloat16),
            pltpu.SMEM((2 + 2 * slots,), jnp.int32),
        ],
        in_specs=[SMEM] + [HBM] * 6 + [VMEM],
        out_specs=[VMEM] * 4 + [SMEM],
        scratch_shapes=[
            pltpu.SMEM((slots,), jnp.int32),
            pltpu.SMEM((slots,), jnp.int32),
            pltpu.SMEM(lengths.shape, jnp.int32),
            pltpu.SemaphoreType.DMA((6,)),
        ],
        compiler_params=params,
        cost_estimate=pl.CostEstimate(
            flops=40_000_000_000, bytes_accessed=60_000_000, transcendentals=0
        ),
        name="spread",
    )(
        me,
        *map(far, (slot_rows, slot_blocks, lengths, queries, new_keys, new_values)),
        lax.ppermute(queries, "inst", core_pairs),
    )
    plan = pltpu.with_memory_space_constraint(plan, pltpu.SMEM)
    asked = over_chips(spread)
    sent_cols = 2 * width + HD
    partial = pl.pallas_call(
        attend_kernel,
        out_shape=jax.ShapeDtypeStruct((steps, sent_cols), jnp.bfloat16),
        in_specs=[SMEM] + [VMEM] * 6,
        out_specs=VMEM,
        scratch_shapes=[
            pltpu.VMEM((2, heads, HD), jnp.bfloat16),
            pltpu.VMEM((slots, heads, block_len), jnp.float32),
        ],
        compiler_params=params,
        cost_estimate=pl.CostEstimate(
            flops=300_000_000, bytes_accessed=9_000_000, transcendentals=600_000
        ),
        name="attend",
    )(
        plan,
        asked,
        near(query),
        near(new_key),
        near(new_value),
        near(key_blocks),
        near(value_blocks),
    )
    everyone = over_chips(jnp.broadcast_to(partial[None], (chips, steps, sent_cols)))
    everyone = everyone.reshape(chips * steps, sent_cols)
    share = pl.pallas_call(
        functools.partial(project_kernel, steps),
        out_shape=jax.ShapeDtypeStruct(
            (shares, devices * steps // shares, out_weight.shape[1]), jnp.bfloat16
        ),
        in_specs=[SMEM] + [VMEM] * 3,
        out_specs=VMEM,
        compiler_params=params,
        name="project",
    )(plan, everyone, lax.ppermute(everyone, "inst", core_pairs), near(out_weight))
    shared = lax.all_to_all(share, "tp", 0, 0, tiled=True)
    return pl.pallas_call(
        add_kernel,
        out_shape=jax.ShapeDtypeStruct(
            (devices // shares, steps, out_weight.shape[1]), jnp.bfloat16
        ),
        in_specs=[VMEM],
        out_specs=VMEM,
        compiler_params=params,
        name="add",
    )(shared)


def solution(mesh):
    in_specs = (
        P("inst", None, "tp"),
        P("inst", None, "tp"),
        P("inst", None, "tp"),
        P("inst", None, "tp"),
        P("inst", None, "tp"),
        P("inst"),
        P("inst"),
        P(),
        P("tp", "inst"),
    )
    out_specs = P("tp", None, "inst")
    return jax.shard_map(body, mesh=mesh, in_specs=in_specs, out_specs=out_specs, check_vma=False)
```

```python
import functools
import math

import jax
import jax.numpy as jnp
from jax import lax
from jax.experimental import pallas as pl
from jax.experimental.pallas import tpu as pltpu
from jax.sharding import PartitionSpec as P

HQ = 8
HD = 128
WIDTH = HQ * HD
NEG = -1e30
FLOOR = -1e29
C = HD ** (-0.5) / math.log(2.0)
PIECES = 3
CORES = 2


def longest_row(lengths_ref):
    row, most = jnp.int32(0), lengths_ref[0]
    for r in range(1, lengths_ref.shape[0]):
        here = lengths_ref[r]
        row = jnp.where(here > most, r, row)
        most = jnp.maximum(here, most)
    return row


def pieces_of(x):
    parts = []
    for _ in range(PIECES):
        part = x.astype(jnp.bfloat16).astype(jnp.float32)
        parts.append(part)
        x = x - part
    return parts


def rows_of_heads(q):
    return jnp.concatenate([q[:, h * HD : (h + 1) * HD] for h in range(HQ)], axis=0)


def plan_kernel(
    block_len,
    me_ref,
    rows_hbm,
    blocks_hbm,
    lengths_hbm,
    query_hbm,
    new_key_hbm,
    new_value_hbm,
    query_ref,
    fresh_ref,
    picks_ref,
    plan_ref,
    rows_ref,
    blocks_ref,
    lengths_ref,
    new_key_ref,
    new_value_ref,
    sems,
):
    slots = rows_ref.shape[0]
    steps = query_ref.shape[0]
    heads = HQ * steps
    copies = [
        pltpu.make_async_copy(source, target, sems.at[k])
        for k, (source, target) in enumerate(
            [
                (lengths_hbm, lengths_ref),
                (query_hbm.at[0], query_ref),
                (rows_hbm, rows_ref),
                (blocks_hbm, blocks_ref),
                (new_key_hbm.at[0], new_key_ref),
                (new_value_hbm.at[0], new_value_ref),
            ]
        )
    ]
    for copy in copies:
        copy.start()

    lane = lax.broadcasted_iota(jnp.int32, (HD, WIDTH), 0)
    chosen = lane % HQ == lax.broadcasted_iota(jnp.int32, (HD, WIDTH), 1) // HD
    split = PIECES * HQ
    picks_ref[0] = jnp.where(chosen & (lane < split), 1.0, 0.0).astype(jnp.bfloat16)
    picks_ref[1] = jnp.where(chosen & (lane >= split), 1.0, 0.0).astype(jnp.bfloat16)

    for copy in copies:
        copy.wait()
    me = me_ref[0]
    longest = longest_row(lengths_ref)
    plan_ref[0] = longest
    plan_ref[1] = me
    for s in range(slots):
        row = rows_ref[s]
        in_long = row == longest
        valid = jnp.clip(lengths_ref[row] - blocks_ref[s] * block_len, 0, block_len)
        plan_ref[2 + s] = in_long.astype(jnp.int32)
        plan_ref[2 + slots + s] = jnp.where(in_long | (row == me), valid, 0)

    query = rows_of_heads(query_ref[...].astype(jnp.float32))
    step_of = lax.broadcasted_iota(jnp.int32, (heads, 1), 0) % steps
    fresh = []
    for u in range(steps):
        score = jnp.sum(
            query * new_key_ref[u : u + 1, :].astype(jnp.float32), axis=1, keepdims=True
        )
        fresh.append(jnp.where(step_of >= u, score, NEG))
    top = functools.reduce(jnp.maximum, fresh)
    total = jnp.zeros_like(top)
    acc = jnp.zeros((heads, HD), jnp.float32)
    for u in range(steps):
        weight = jnp.exp2((fresh[u] - top) * C)
        total += weight
        acc += weight.astype(jnp.bfloat16).astype(jnp.float32) * new_value_ref[
            u : u + 1, :
        ].astype(jnp.float32)
    fresh_ref[0] = jnp.broadcast_to(top, (heads, HD))
    fresh_ref[1] = jnp.broadcast_to(total, (heads, HD))
    fresh_ref[2] = acc


def spread_kernel(plan_ref, query_ref, other_ref, spread_ref):
    me = plan_ref[1]
    asked = jnp.where(
        me + 1 - 2 * (me % CORES) == plan_ref[0],
        other_ref[0].astype(jnp.float32),
        query_ref[...].astype(jnp.float32),
    ).astype(jnp.bfloat16)
    spread_ref[...] = jnp.broadcast_to(asked[None], spread_ref.shape)


def attend_kernel(
    plan_ref,
    asked_ref,
    query_ref,
    fresh_ref,
    key_ref,
    value_ref,
    out_ref,
    queries,
    scores,
):
    slots, block_len, _ = key_ref.shape
    steps = query_ref.shape[0]
    heads = HQ * steps
    longest = plan_ref[0]
    mine = plan_ref[1] == longest
    queries[0] = rows_of_heads(query_ref[...].astype(jnp.float32)).astype(jnp.bfloat16)
    queries[1] = rows_of_heads(asked_ref[longest // CORES].astype(jnp.float32)).astype(jnp.bfloat16)

    column = lax.broadcasted_iota(jnp.int32, (heads, block_len), 1)
    tops = []
    for s in range(slots):
        score = lax.dot_general(
            queries[plan_ref[2 + s]],
            key_ref[s],
            (((1,), (1,)), ((), ())),
            preferred_element_type=jnp.float32,
        )
        score = jnp.where(column < plan_ref[2 + slots + s], score, NEG)
        scores[s] = score
        tops.append(jnp.maximum(jnp.max(score, axis=1, keepdims=True), FLOOR))

    parts = [(mine, fresh_ref[0][:, :1], fresh_ref[1][:, :1], fresh_ref[2])]

    for s in range(slots):
        weights = jnp.exp2((scores[s] - tops[s]) * C)
        total = jnp.sum(weights, axis=1, keepdims=True)
        acc = jnp.dot(
            weights.astype(jnp.bfloat16), value_ref[s], preferred_element_type=jnp.float32
        )
        parts.append((plan_ref[2 + s] == 1, tops[s], total, acc))

    merged = []
    for wanted in (False, True):
        best = functools.reduce(
            jnp.maximum, [jnp.where(in_long == wanted, top, FLOOR) for in_long, top, _, _ in parts]
        )
        sum_all = jnp.zeros_like(best)
        acc_all = jnp.zeros((heads, HD), jnp.float32)
        for in_long, top, total, acc in parts:
            factor = jnp.where(in_long == wanted, jnp.exp2(jnp.minimum(top - best, 0.0) * C), 0.0)
            sum_all += factor * total
            acc_all += factor * acc
        merged.append((best, sum_all, acc_all))

    _, own_sum, own_acc = merged[0]
    attended = own_acc / jnp.where(own_sum > 0.0, own_sum, 1.0)
    long_top, long_sum, long_acc = merged[1]
    stats = pieces_of(long_top) + pieces_of(long_sum)
    lane = lax.broadcasted_iota(jnp.int32, (steps, HD), 1)
    packed = jnp.zeros((steps, HD), jnp.float32)
    for h in range(HQ):
        rows = slice(h * steps, (h + 1) * steps)
        for k, piece in enumerate(stats):
            packed = jnp.where(lane == k * HQ + h, piece[rows], packed)
    heads_of = lambda x: [x[h * steps : (h + 1) * steps] for h in range(HQ)]
    sent = jnp.concatenate(heads_of(attended) + heads_of(long_acc) + [packed], axis=1)
    out_ref[...] = jnp.broadcast_to(sent.astype(jnp.bfloat16)[None], out_ref.shape)


def project_kernel(steps, plan_ref, picks_ref, mine_ref, other_ref, weight_ref, out_ref):
    half, _ = mine_ref.shape
    rows = CORES * half
    longest = plan_ref[0]
    first = plan_ref[1] % CORES == 0
    both = lambda cols: jnp.concatenate([mine_ref[:, cols], other_ref[:, cols]], axis=0)
    stats = both(slice(2 * WIDTH, 2 * WIDTH + HD))
    tops = jnp.dot(stats, picks_ref[0], preferred_element_type=jnp.float32)
    sums = jnp.dot(stats, picks_ref[1], preferred_element_type=jnp.float32)
    accs = both(slice(WIDTH, 2 * WIDTH)).astype(jnp.float32)

    pair = 2 * steps
    fold = lambda x: x.reshape(-1, pair, x.shape[-1])
    best = jnp.max(fold(tops), axis=0)
    best = jnp.maximum(best, pltpu.roll(best, steps, 0))
    factor = jnp.exp2((fold(tops) - best[None]) * C)
    total = jnp.sum(factor * fold(sums), axis=0)
    weighted = jnp.sum(factor * fold(accs), axis=0)
    total = total + pltpu.roll(total, steps, 0)
    weighted = weighted + pltpu.roll(weighted, steps, 0)
    merged = weighted / total

    own = mine_ref[:, :WIDTH].astype(jnp.float32)
    other = other_ref[:, :WIDTH].astype(jnp.float32)
    own, other = jnp.where(first, own, other), jnp.where(first, other, own)
    shape = (half // pair, pair, WIDTH)
    chip = lax.broadcasted_iota(jnp.int32, shape, 0) * (pair // steps)
    chip = chip + lax.broadcasted_iota(jnp.int32, shape, 1) // steps
    attended = [
        jnp.where(chip * CORES + core == longest, merged[None], fold(part)).reshape(half, WIDTH)
        for core, part in enumerate((own, other))
    ]
    product = jnp.dot(
        jnp.concatenate(attended, axis=0).astype(jnp.bfloat16),
        weight_ref[...],
        preferred_element_type=jnp.float32,
    )
    shares, each, cols = out_ref.shape
    product = product.reshape(CORES, shares, each // CORES, cols)
    out_ref[...] = jnp.concatenate([product[c] for c in range(CORES)], axis=1).astype(out_ref.dtype)


def add_kernel(shares_ref, out_ref):
    rows, steps, _ = out_ref.shape
    summed = jnp.sum(shares_ref[...].astype(jnp.float32), axis=0)
    for core in range(CORES):
        for k in range(rows // CORES):
            at = (core * (rows // CORES) + k) * steps
            out_ref[k * CORES + core] = summed[at : at + steps].astype(out_ref.dtype)


SMEM = pl.BlockSpec(memory_space=pltpu.SMEM)
VMEM = pl.BlockSpec(memory_space=pltpu.VMEM)
HBM = pl.BlockSpec(memory_space=pltpu.HBM)


def near(x):
    return pltpu.with_memory_space_constraint(x, pltpu.VMEM)


def far(x):
    return pltpu.with_memory_space_constraint(x, pltpu.HBM)


def body(
    queries,
    new_keys,
    new_values,
    key_blocks,
    value_blocks,
    slot_rows,
    slot_blocks,
    lengths,
    out_weight,
):
    _, steps, width = queries.shape
    slots, block_len, _ = key_blocks.shape
    heads = HQ * steps
    devices = lax.axis_size("inst")
    chips = devices // CORES
    shares = lax.axis_size("tp")
    me = lax.axis_index("inst").astype(jnp.int32).reshape(1)
    same_core = [[chip * CORES + core for chip in range(chips)] for core in range(CORES)]
    core_pairs = [(i, i ^ 1) for i in range(devices)]
    params = pltpu.CompilerParams(vmem_limit_bytes=24 * 1024 * 1024)

    def over_chips(x):
        return lax.all_to_all(x, "inst", 0, 0, tiled=True, axis_index_groups=same_core)

    other = lax.ppermute(queries, "inst", core_pairs)
    query, fresh, picks, plan = pl.pallas_call(
        functools.partial(plan_kernel, block_len),
        out_shape=[
            pltpu.VMEM((steps, width), jnp.bfloat16),
            pltpu.VMEM((3, heads, HD), jnp.float32),
            pltpu.VMEM((2, HD, width), jnp.bfloat16),
            pltpu.SMEM((2 + 2 * slots,), jnp.int32),
        ],
        in_specs=[SMEM] + [HBM] * 6,
        out_specs=[VMEM] * 3 + [SMEM],
        scratch_shapes=[
            pltpu.SMEM((slots,), jnp.int32),
            pltpu.SMEM((slots,), jnp.int32),
            pltpu.SMEM(lengths.shape, jnp.int32),
            pltpu.VMEM((steps, HD), jnp.bfloat16),
            pltpu.VMEM((steps, HD), jnp.bfloat16),
            pltpu.SemaphoreType.DMA((6,)),
        ],
        compiler_params=params,
        cost_estimate=pl.CostEstimate(flops=1_000_000, bytes_accessed=3_000_000, transcendentals=0),
        name="plan",
    )(me, *map(far, (slot_rows, slot_blocks, lengths, queries, new_keys, new_values)))
    plan = pltpu.with_memory_space_constraint(plan, pltpu.SMEM)
    picks = near(picks)
    spread = pl.pallas_call(
        spread_kernel,
        out_shape=pltpu.VMEM((chips, steps, width), jnp.bfloat16),
        in_specs=[SMEM, VMEM, VMEM],
        out_specs=VMEM,
        compiler_params=params,
        cost_estimate=pl.CostEstimate(
            flops=40_000_000_000, bytes_accessed=60_000_000, transcendentals=0
        ),
        name="spread",
    )(plan, near(query), other)
    asked = over_chips(spread)
    sent_cols = 2 * width + HD
    partial = pl.pallas_call(
        attend_kernel,
        out_shape=pltpu.VMEM((chips, steps, sent_cols), jnp.bfloat16),
        in_specs=[SMEM] + [VMEM] * 5,
        out_specs=VMEM,
        scratch_shapes=[
            pltpu.VMEM((2, heads, HD), jnp.bfloat16),
            pltpu.VMEM((slots, heads, block_len), jnp.float32),
        ],
        compiler_params=params,
        cost_estimate=pl.CostEstimate(
            flops=300_000_000, bytes_accessed=9_000_000, transcendentals=600_000
        ),
        name="attend",
    )(plan, asked, near(query), near(fresh), near(key_blocks), near(value_blocks))
    everyone = over_chips(partial)
    everyone = everyone.reshape(chips * steps, sent_cols)
    share = pl.pallas_call(
        functools.partial(project_kernel, steps),
        out_shape=jax.ShapeDtypeStruct(
            (shares, devices * steps // shares, out_weight.shape[1]), jnp.bfloat16
        ),
        in_specs=[SMEM] + [VMEM] * 4,
        out_specs=VMEM,
        compiler_params=params,
        name="project",
    )(plan, picks, everyone, lax.ppermute(everyone, "inst", core_pairs), near(out_weight))
    shared = lax.all_to_all(share, "tp", 0, 0, tiled=True)
    return pl.pallas_call(
        add_kernel,
        out_shape=jax.ShapeDtypeStruct(
            (devices // shares, steps, out_weight.shape[1]), jnp.bfloat16
        ),
        in_specs=[VMEM],
        out_specs=VMEM,
        compiler_params=params,
        name="add",
    )(shared)


def solution(mesh):
    in_specs = (
        P("inst", None, "tp"),
        P("inst", None, "tp"),
        P("inst", None, "tp"),
        P("inst", None, "tp"),
        P("inst", None, "tp"),
        P("inst"),
        P("inst"),
        P(),
        P("tp", "inst"),
    )
    out_specs = P("tp", None, "inst")
    return jax.shard_map(body, mesh=mesh, in_specs=in_specs, out_specs=out_specs, check_vma=False)
```

```python
import functools
import math

import jax
import jax.numpy as jnp
from jax import lax
from jax.experimental import pallas as pl
from jax.experimental.pallas import tpu as pltpu
from jax.sharding import PartitionSpec as P

HQ = 8
HD = 128
WIDTH = HQ * HD
NEG = -1e30
FLOOR = -1e29
C = HD ** (-0.5) / math.log(2.0)
PIECES = 3
CORES = 2
CHIP_ORDER = [2, 14, 12, 9, 0, 3, 4, 10, 11, 5, 15, 8, 13, 7, 6, 1]
TP_ORDER = [0, 2, 4, 6, 1, 3, 5, 7]


def longest_row(lengths_ref):
    row, most = jnp.int32(0), lengths_ref[0]
    for r in range(1, lengths_ref.shape[0]):
        here = lengths_ref[r]
        row = jnp.where(here > most, r, row)
        most = jnp.maximum(here, most)
    return row


def pieces_of(x):
    parts = []
    for _ in range(PIECES):
        part = x.astype(jnp.bfloat16).astype(jnp.float32)
        parts.append(part)
        x = x - part
    return parts


def rows_of_heads(q):
    return jnp.concatenate([q[:, h * HD : (h + 1) * HD] for h in range(HQ)], axis=0)


def plan_kernel(
    block_len,
    me_ref,
    rows_hbm,
    blocks_hbm,
    lengths_hbm,
    query_hbm,
    new_key_hbm,
    new_value_hbm,
    query_ref,
    fresh_ref,
    picks_ref,
    plan_ref,
    rows_ref,
    blocks_ref,
    lengths_ref,
    new_key_ref,
    new_value_ref,
    sems,
):
    slots = rows_ref.shape[0]
    steps = query_ref.shape[0]
    heads = HQ * steps
    copies = [
        pltpu.make_async_copy(source, target, sems.at[k])
        for k, (source, target) in enumerate(
            [
                (lengths_hbm, lengths_ref),
                (query_hbm.at[0], query_ref),
                (rows_hbm, rows_ref),
                (blocks_hbm, blocks_ref),
                (new_key_hbm.at[0], new_key_ref),
                (new_value_hbm.at[0], new_value_ref),
            ]
        )
    ]
    for copy in copies:
        copy.start()

    lane = lax.broadcasted_iota(jnp.int32, (HD, WIDTH), 0)
    chosen = lane % HQ == lax.broadcasted_iota(jnp.int32, (HD, WIDTH), 1) // HD
    split = PIECES * HQ
    picks_ref[0] = jnp.where(chosen & (lane < split), 1.0, 0.0).astype(jnp.bfloat16)
    picks_ref[1] = jnp.where(chosen & (lane >= split), 1.0, 0.0).astype(jnp.bfloat16)

    for copy in copies:
        copy.wait()
    me = me_ref[0]
    longest = longest_row(lengths_ref)
    plan_ref[0] = longest
    plan_ref[1] = me
    place = jnp.int32(0)
    for k, chip in enumerate(CHIP_ORDER):
        place = jnp.where(longest // CORES == chip, k, place)
    plan_ref[2 + 2 * slots] = place
    for s in range(slots):
        row = rows_ref[s]
        in_long = row == longest
        valid = jnp.clip(lengths_ref[row] - blocks_ref[s] * block_len, 0, block_len)
        plan_ref[2 + s] = in_long.astype(jnp.int32)
        plan_ref[2 + slots + s] = jnp.where(in_long | (row == me), valid, 0)

    query = rows_of_heads(query_ref[...].astype(jnp.float32))
    step_of = lax.broadcasted_iota(jnp.int32, (heads, 1), 0) % steps
    fresh = []
    for u in range(steps):
        score = jnp.sum(
            query * new_key_ref[u : u + 1, :].astype(jnp.float32), axis=1, keepdims=True
        )
        fresh.append(jnp.where(step_of >= u, score, NEG))
    top = functools.reduce(jnp.maximum, fresh)
    total = jnp.zeros_like(top)
    acc = jnp.zeros((heads, HD), jnp.float32)
    for u in range(steps):
        weight = jnp.exp2((fresh[u] - top) * C)
        total += weight
        acc += weight.astype(jnp.bfloat16).astype(jnp.float32) * new_value_ref[
            u : u + 1, :
        ].astype(jnp.float32)
    fresh_ref[0] = jnp.broadcast_to(top, (heads, HD))
    fresh_ref[1] = jnp.broadcast_to(total, (heads, HD))
    fresh_ref[2] = acc


def spread_kernel(plan_ref, query_ref, other_ref, spread_ref):
    me = plan_ref[1]
    asked = jnp.where(
        me + 1 - 2 * (me % CORES) == plan_ref[0],
        other_ref[0].astype(jnp.float32),
        query_ref[...].astype(jnp.float32),
    ).astype(jnp.bfloat16)
    spread_ref[...] = jnp.broadcast_to(asked[None], spread_ref.shape)


def attend_kernel(
    plan_ref,
    asked_ref,
    query_ref,
    fresh_ref,
    key_ref,
    value_ref,
    out_ref,
    queries,
    scores,
):
    slots, block_len, _ = key_ref.shape
    steps = query_ref.shape[0]
    heads = HQ * steps
    longest = plan_ref[0]
    mine = plan_ref[1] == longest
    queries[0] = rows_of_heads(query_ref[...].astype(jnp.float32)).astype(jnp.bfloat16)
    queries[1] = rows_of_heads(asked_ref[plan_ref[2 + 2 * slots]].astype(jnp.float32)).astype(jnp.bfloat16)

    column = lax.broadcasted_iota(jnp.int32, (heads, block_len), 1)
    tops = []
    for s in range(slots):
        score = lax.dot_general(
            queries[plan_ref[2 + s]],
            key_ref[s],
            (((1,), (1,)), ((), ())),
            preferred_element_type=jnp.float32,
        )
        score = jnp.where(column < plan_ref[2 + slots + s], score, NEG)
        scores[s] = score
        tops.append(jnp.maximum(jnp.max(score, axis=1, keepdims=True), FLOOR))

    parts = [(mine, fresh_ref[0][:, :1], fresh_ref[1][:, :1], fresh_ref[2])]

    for s in range(slots):
        weights = jnp.exp2((scores[s] - tops[s]) * C)
        total = jnp.sum(weights, axis=1, keepdims=True)
        acc = jnp.dot(
            weights.astype(jnp.bfloat16), value_ref[s], preferred_element_type=jnp.float32
        )
        parts.append((plan_ref[2 + s] == 1, tops[s], total, acc))

    merged = []
    for wanted in (False, True):
        best = functools.reduce(
            jnp.maximum, [jnp.where(in_long == wanted, top, FLOOR) for in_long, top, _, _ in parts]
        )
        sum_all = jnp.zeros_like(best)
        acc_all = jnp.zeros((heads, HD), jnp.float32)
        for in_long, top, total, acc in parts:
            factor = jnp.where(in_long == wanted, jnp.exp2(jnp.minimum(top - best, 0.0) * C), 0.0)
            sum_all += factor * total
            acc_all += factor * acc
        merged.append((best, sum_all, acc_all))

    _, own_sum, own_acc = merged[0]
    attended = own_acc / jnp.where(own_sum > 0.0, own_sum, 1.0)
    long_top, long_sum, long_acc = merged[1]
    stats = pieces_of(long_top) + pieces_of(long_sum)
    lane = lax.broadcasted_iota(jnp.int32, (steps, HD), 1)
    packed = jnp.zeros((steps, HD), jnp.float32)
    for h in range(HQ):
        rows = slice(h * steps, (h + 1) * steps)
        for k, piece in enumerate(stats):
            packed = jnp.where(lane == k * HQ + h, piece[rows], packed)
    heads_of = lambda x: [x[h * steps : (h + 1) * steps] for h in range(HQ)]
    sent = jnp.concatenate(heads_of(attended) + heads_of(long_acc) + [packed], axis=1)
    out_ref[...] = jnp.broadcast_to(sent.astype(jnp.bfloat16)[None], out_ref.shape)


def project_kernel(steps, place_at, plan_ref, picks_ref, mine_ref, other_ref, weight_ref, out_ref):
    half, _ = mine_ref.shape
    rows = CORES * half
    longest = plan_ref[0]
    first = plan_ref[1] % CORES == 0
    both = lambda cols: jnp.concatenate([mine_ref[:, cols], other_ref[:, cols]], axis=0)
    stats = both(slice(2 * WIDTH, 2 * WIDTH + HD))
    tops = jnp.dot(stats, picks_ref[0], preferred_element_type=jnp.float32)
    sums = jnp.dot(stats, picks_ref[1], preferred_element_type=jnp.float32)
    accs = both(slice(WIDTH, 2 * WIDTH)).astype(jnp.float32)

    pair = 2 * steps
    fold = lambda x: x.reshape(-1, pair, x.shape[-1])
    best = jnp.max(fold(tops), axis=0)
    best = jnp.maximum(best, pltpu.roll(best, steps, 0))
    factor = jnp.exp2((fold(tops) - best[None]) * C)
    total = jnp.sum(factor * fold(sums), axis=0)
    weighted = jnp.sum(factor * fold(accs), axis=0)
    total = total + pltpu.roll(total, steps, 0)
    weighted = weighted + pltpu.roll(weighted, steps, 0)
    merged = weighted / total

    own = mine_ref[:, :WIDTH].astype(jnp.float32)
    other = other_ref[:, :WIDTH].astype(jnp.float32)
    own, other = jnp.where(first, own, other), jnp.where(first, other, own)
    shape = (half // pair, pair, WIDTH)
    place = lax.broadcasted_iota(jnp.int32, shape, 0) * (pair // steps)
    place = place + lax.broadcasted_iota(jnp.int32, shape, 1) // steps
    attended = []
    for core, part in enumerate((own, other)):
        wanted = jnp.where(longest % CORES == core, plan_ref[place_at], -1)
        attended.append(jnp.where(place == wanted, merged[None], fold(part)).reshape(half, WIDTH))
    product = jnp.dot(
        jnp.concatenate(attended, axis=0).astype(jnp.bfloat16),
        weight_ref[...],
        preferred_element_type=jnp.float32,
    )
    shares, each, _ = out_ref.shape
    chips = each // (CORES * steps)
    for k, share in enumerate(TP_ORDER):
        starts = [
            core * half + CHIP_ORDER.index(share * chips + chip) * steps
            for core in range(CORES)
            for chip in range(chips)
        ]
        rows = jnp.concatenate([product[at : at + steps] for at in starts], axis=0)
        out_ref[k] = rows.astype(out_ref.dtype)


def add_kernel(shares_ref, out_ref):
    rows, steps, _ = out_ref.shape
    summed = jnp.sum(shares_ref[...].astype(jnp.float32), axis=0)
    for core in range(CORES):
        for k in range(rows // CORES):
            at = (core * (rows // CORES) + k) * steps
            out_ref[k * CORES + core] = summed[at : at + steps].astype(out_ref.dtype)


SMEM = pl.BlockSpec(memory_space=pltpu.SMEM)
VMEM = pl.BlockSpec(memory_space=pltpu.VMEM)
HBM = pl.BlockSpec(memory_space=pltpu.HBM)


def near(x):
    return pltpu.with_memory_space_constraint(x, pltpu.VMEM)


def far(x):
    return pltpu.with_memory_space_constraint(x, pltpu.HBM)


def body(
    queries,
    new_keys,
    new_values,
    key_blocks,
    value_blocks,
    slot_rows,
    slot_blocks,
    lengths,
    out_weight,
):
    _, steps, width = queries.shape
    slots, block_len, _ = key_blocks.shape
    heads = HQ * steps
    devices = lax.axis_size("inst")
    chips = devices // CORES
    shares = lax.axis_size("tp")
    me = lax.axis_index("inst").astype(jnp.int32).reshape(1)
    same_core = [[chip * CORES + core for chip in CHIP_ORDER] for core in range(CORES)]
    core_pairs = [(i, i ^ 1) for i in range(devices)]
    params = pltpu.CompilerParams(vmem_limit_bytes=24 * 1024 * 1024)

    def over_chips(x):
        return lax.all_to_all(x, "inst", 0, 0, tiled=True, axis_index_groups=same_core)

    other = lax.ppermute(queries, "inst", core_pairs)
    query, fresh, picks, plan = pl.pallas_call(
        functools.partial(plan_kernel, block_len),
        out_shape=[
            pltpu.VMEM((steps, width), jnp.bfloat16),
            pltpu.VMEM((3, heads, HD), jnp.float32),
            pltpu.VMEM((2, HD, width), jnp.bfloat16),
            pltpu.SMEM((3 + 2 * slots,), jnp.int32),
        ],
        in_specs=[SMEM] + [HBM] * 6,
        out_specs=[VMEM] * 3 + [SMEM],
        scratch_shapes=[
            pltpu.SMEM((slots,), jnp.int32),
            pltpu.SMEM((slots,), jnp.int32),
            pltpu.SMEM(lengths.shape, jnp.int32),
            pltpu.VMEM((steps, HD), jnp.bfloat16),
            pltpu.VMEM((steps, HD), jnp.bfloat16),
            pltpu.SemaphoreType.DMA((6,)),
        ],
        compiler_params=params,
        cost_estimate=pl.CostEstimate(flops=1_000_000, bytes_accessed=3_000_000, transcendentals=0),
        name="plan",
    )(me, *map(far, (slot_rows, slot_blocks, lengths, queries, new_keys, new_values)))
    plan = pltpu.with_memory_space_constraint(plan, pltpu.SMEM)
    picks = near(picks)
    spread = pl.pallas_call(
        spread_kernel,
        out_shape=pltpu.VMEM((chips, steps, width), jnp.bfloat16),
        in_specs=[SMEM, VMEM, VMEM],
        out_specs=VMEM,
        compiler_params=params,
        cost_estimate=pl.CostEstimate(
            flops=40_000_000_000, bytes_accessed=60_000_000, transcendentals=0
        ),
        name="spread",
    )(plan, near(query), other)
    asked = over_chips(spread)
    sent_cols = 2 * width + HD
    partial = pl.pallas_call(
        attend_kernel,
        out_shape=pltpu.VMEM((chips, steps, sent_cols), jnp.bfloat16),
        in_specs=[SMEM] + [VMEM] * 5,
        out_specs=VMEM,
        scratch_shapes=[
            pltpu.VMEM((2, heads, HD), jnp.bfloat16),
            pltpu.VMEM((slots, heads, block_len), jnp.float32),
        ],
        compiler_params=params,
        cost_estimate=pl.CostEstimate(
            flops=300_000_000, bytes_accessed=9_000_000, transcendentals=600_000
        ),
        name="attend",
    )(plan, asked, near(query), near(fresh), near(key_blocks), near(value_blocks))
    everyone = over_chips(partial)
    everyone = everyone.reshape(chips * steps, sent_cols)
    share = pl.pallas_call(
        functools.partial(project_kernel, steps, 2 + 2 * slots),
        out_shape=jax.ShapeDtypeStruct(
            (shares, devices * steps // shares, out_weight.shape[1]), jnp.bfloat16
        ),
        in_specs=[SMEM] + [VMEM] * 4,
        out_specs=VMEM,
        compiler_params=params,
        name="project",
    )(plan, picks, everyone, lax.ppermute(everyone, "inst", core_pairs), near(out_weight))
    shared = lax.all_to_all(share, "tp", 0, 0, tiled=True, axis_index_groups=[TP_ORDER])
    return pl.pallas_call(
        add_kernel,
        out_shape=jax.ShapeDtypeStruct(
            (devices // shares, steps, out_weight.shape[1]), jnp.bfloat16
        ),
        in_specs=[VMEM],
        out_specs=VMEM,
        compiler_params=params,
        name="add",
    )(shared)


def solution(mesh):
    in_specs = (
        P("inst", None, "tp"),
        P("inst", None, "tp"),
        P("inst", None, "tp"),
        P("inst", None, "tp"),
        P("inst", None, "tp"),
        P("inst"),
        P("inst"),
        P(),
        P("tp", "inst"),
    )
    out_specs = P("tp", None, "inst")
    return jax.shard_map(body, mesh=mesh, in_specs=in_specs, out_specs=out_specs, check_vma=False)
```

```python
import functools
import math

import jax
import jax.numpy as jnp
from jax import lax
from jax.experimental import pallas as pl
from jax.experimental.pallas import tpu as pltpu
from jax.sharding import PartitionSpec as P

HQ = 8
HD = 128
WIDTH = HQ * HD
NEG = -1e30
FLOOR = -1e29
C = HD ** (-0.5) / math.log(2.0)
PIECES = 3
CORES = 2
ASK_ORDER = [10, 11, 8, 9, 15, 12, 13, 14, 0, 1, 2, 3, 5, 6, 7, 4]
SEND_ORDER = [10, 11, 5, 15, 8, 13, 7, 6, 1, 2, 14, 12, 9, 0, 3, 4]
TP_ORDER = [4, 6, 1, 3, 5, 7, 0, 2]


def longest_row(lengths_ref):
    row, most = jnp.int32(0), lengths_ref[0]
    for r in range(1, lengths_ref.shape[0]):
        here = lengths_ref[r]
        row = jnp.where(here > most, r, row)
        most = jnp.maximum(here, most)
    return row


def pieces_of(x):
    parts = []
    for _ in range(PIECES):
        part = x.astype(jnp.bfloat16).astype(jnp.float32)
        parts.append(part)
        x = x - part
    return parts


def rows_of_heads(q):
    return jnp.concatenate([q[:, h * HD : (h + 1) * HD] for h in range(HQ)], axis=0)


def plan_kernel(
    block_len,
    me_ref,
    rows_hbm,
    blocks_hbm,
    lengths_hbm,
    query_hbm,
    new_key_hbm,
    new_value_hbm,
    query_ref,
    fresh_ref,
    picks_ref,
    plan_ref,
    rows_ref,
    blocks_ref,
    lengths_ref,
    new_key_ref,
    new_value_ref,
    sems,
):
    slots = rows_ref.shape[0]
    steps = query_ref.shape[0]
    heads = HQ * steps
    copies = [
        pltpu.make_async_copy(source, target, sems.at[k])
        for k, (source, target) in enumerate(
            [
                (lengths_hbm, lengths_ref),
                (query_hbm.at[0], query_ref),
                (rows_hbm, rows_ref),
                (blocks_hbm, blocks_ref),
                (new_key_hbm.at[0], new_key_ref),
                (new_value_hbm.at[0], new_value_ref),
            ]
        )
    ]
    for copy in copies:
        copy.start()

    lane = lax.broadcasted_iota(jnp.int32, (HD, WIDTH), 0)
    chosen = lane % HQ == lax.broadcasted_iota(jnp.int32, (HD, WIDTH), 1) // HD
    split = PIECES * HQ
    picks_ref[0] = jnp.where(chosen & (lane < split), 1.0, 0.0).astype(jnp.bfloat16)
    picks_ref[1] = jnp.where(chosen & (lane >= split), 1.0, 0.0).astype(jnp.bfloat16)

    for copy in copies:
        copy.wait()
    me = me_ref[0]
    longest = longest_row(lengths_ref)
    plan_ref[0] = longest
    plan_ref[1] = me
    for at, order in enumerate((ASK_ORDER, SEND_ORDER)):
        place = jnp.int32(0)
        for k, chip in enumerate(order):
            place = jnp.where(longest // CORES == chip, k, place)
        plan_ref[2 + 2 * slots + at] = place
    for s in range(slots):
        row = rows_ref[s]
        in_long = row == longest
        valid = jnp.clip(lengths_ref[row] - blocks_ref[s] * block_len, 0, block_len)
        plan_ref[2 + s] = in_long.astype(jnp.int32)
        plan_ref[2 + slots + s] = jnp.where(in_long | (row == me), valid, 0)

    query = rows_of_heads(query_ref[...].astype(jnp.float32))
    step_of = lax.broadcasted_iota(jnp.int32, (heads, 1), 0) % steps
    fresh = []
    for u in range(steps):
        score = jnp.sum(
            query * new_key_ref[u : u + 1, :].astype(jnp.float32), axis=1, keepdims=True
        )
        fresh.append(jnp.where(step_of >= u, score, NEG))
    top = functools.reduce(jnp.maximum, fresh)
    total = jnp.zeros_like(top)
    acc = jnp.zeros((heads, HD), jnp.float32)
    for u in range(steps):
        weight = jnp.exp2((fresh[u] - top) * C)
        total += weight
        acc += weight.astype(jnp.bfloat16).astype(jnp.float32) * new_value_ref[
            u : u + 1, :
        ].astype(jnp.float32)
    fresh_ref[0] = jnp.broadcast_to(top, (heads, HD))
    fresh_ref[1] = jnp.broadcast_to(total, (heads, HD))
    fresh_ref[2] = acc


def spread_kernel(plan_ref, query_ref, other_ref, spread_ref):
    me = plan_ref[1]
    asked = jnp.where(
        me + 1 - 2 * (me % CORES) == plan_ref[0],
        other_ref[0].astype(jnp.float32),
        query_ref[...].astype(jnp.float32),
    ).astype(jnp.bfloat16)
    spread_ref[...] = jnp.broadcast_to(asked[None], spread_ref.shape)


def attend_kernel(
    plan_ref,
    asked_ref,
    query_ref,
    fresh_ref,
    key_ref,
    value_ref,
    out_ref,
    queries,
    scores,
):
    slots, block_len, _ = key_ref.shape
    steps = query_ref.shape[0]
    heads = HQ * steps
    longest = plan_ref[0]
    mine = plan_ref[1] == longest
    queries[0] = rows_of_heads(query_ref[...].astype(jnp.float32)).astype(jnp.bfloat16)
    queries[1] = rows_of_heads(asked_ref[plan_ref[2 + 2 * slots]].astype(jnp.float32)).astype(jnp.bfloat16)

    column = lax.broadcasted_iota(jnp.int32, (heads, block_len), 1)
    tops = []
    for s in range(slots):
        score = lax.dot_general(
            queries[plan_ref[2 + s]],
            key_ref[s],
            (((1,), (1,)), ((), ())),
            preferred_element_type=jnp.float32,
        )
        score = jnp.where(column < plan_ref[2 + slots + s], score, NEG)
        scores[s] = score
        tops.append(jnp.maximum(jnp.max(score, axis=1, keepdims=True), FLOOR))

    parts = [(mine, fresh_ref[0][:, :1], fresh_ref[1][:, :1], fresh_ref[2])]

    for s in range(slots):
        weights = jnp.exp2((scores[s] - tops[s]) * C)
        total = jnp.sum(weights, axis=1, keepdims=True)
        acc = jnp.dot(
            weights.astype(jnp.bfloat16), value_ref[s], preferred_element_type=jnp.float32
        )
        parts.append((plan_ref[2 + s] == 1, tops[s], total, acc))

    merged = []
    for wanted in (False, True):
        best = functools.reduce(
            jnp.maximum, [jnp.where(in_long == wanted, top, FLOOR) for in_long, top, _, _ in parts]
        )
        sum_all = jnp.zeros_like(best)
        acc_all = jnp.zeros((heads, HD), jnp.float32)
        for in_long, top, total, acc in parts:
            factor = jnp.where(in_long == wanted, jnp.exp2(jnp.minimum(top - best, 0.0) * C), 0.0)
            sum_all += factor * total
            acc_all += factor * acc
        merged.append((best, sum_all, acc_all))

    _, own_sum, own_acc = merged[0]
    attended = own_acc / jnp.where(own_sum > 0.0, own_sum, 1.0)
    long_top, long_sum, long_acc = merged[1]
    stats = pieces_of(long_top) + pieces_of(long_sum)
    lane = lax.broadcasted_iota(jnp.int32, (steps, HD), 1)
    packed = jnp.zeros((steps, HD), jnp.float32)
    for h in range(HQ):
        rows = slice(h * steps, (h + 1) * steps)
        for k, piece in enumerate(stats):
            packed = jnp.where(lane == k * HQ + h, piece[rows], packed)
    heads_of = lambda x: [x[h * steps : (h + 1) * steps] for h in range(HQ)]
    sent = jnp.concatenate(heads_of(attended) + heads_of(long_acc) + [packed], axis=1)
    out_ref[...] = jnp.broadcast_to(sent.astype(jnp.bfloat16)[None], out_ref.shape)


def project_kernel(steps, place_at, plan_ref, picks_ref, mine_ref, other_ref, weight_ref, out_ref):
    half, _ = mine_ref.shape
    rows = CORES * half
    longest = plan_ref[0]
    first = plan_ref[1] % CORES == 0
    both = lambda cols: jnp.concatenate([mine_ref[:, cols], other_ref[:, cols]], axis=0)
    stats = both(slice(2 * WIDTH, 2 * WIDTH + HD))
    tops = jnp.dot(stats, picks_ref[0], preferred_element_type=jnp.float32)
    sums = jnp.dot(stats, picks_ref[1], preferred_element_type=jnp.float32)
    accs = both(slice(WIDTH, 2 * WIDTH)).astype(jnp.float32)

    pair = 2 * steps
    fold = lambda x: x.reshape(-1, pair, x.shape[-1])
    best = jnp.max(fold(tops), axis=0)
    best = jnp.maximum(best, pltpu.roll(best, steps, 0))
    factor = jnp.exp2((fold(tops) - best[None]) * C)
    total = jnp.sum(factor * fold(sums), axis=0)
    weighted = jnp.sum(factor * fold(accs), axis=0)
    total = total + pltpu.roll(total, steps, 0)
    weighted = weighted + pltpu.roll(weighted, steps, 0)
    merged = weighted / total

    own = mine_ref[:, :WIDTH].astype(jnp.float32)
    other = other_ref[:, :WIDTH].astype(jnp.float32)
    own, other = jnp.where(first, own, other), jnp.where(first, other, own)
    shape = (half // pair, pair, WIDTH)
    place = lax.broadcasted_iota(jnp.int32, shape, 0) * (pair // steps)
    place = place + lax.broadcasted_iota(jnp.int32, shape, 1) // steps
    attended = []
    for core, part in enumerate((own, other)):
        wanted = jnp.where(longest % CORES == core, plan_ref[place_at], -1)
        attended.append(jnp.where(place == wanted, merged[None], fold(part)).reshape(half, WIDTH))
    product = jnp.dot(
        jnp.concatenate(attended, axis=0).astype(jnp.bfloat16),
        weight_ref[...],
        preferred_element_type=jnp.float32,
    )
    shares, each, _ = out_ref.shape
    chips = each // (CORES * steps)
    for k, share in enumerate(TP_ORDER):
        starts = [
            core * half + SEND_ORDER.index(share * chips + chip) * steps
            for core in range(CORES)
            for chip in range(chips)
        ]
        rows = jnp.concatenate([product[at : at + steps] for at in starts], axis=0)
        out_ref[k] = rows.astype(out_ref.dtype)


def add_kernel(shares_ref, out_ref):
    rows, steps, _ = out_ref.shape
    summed = jnp.sum(shares_ref[...].astype(jnp.float32), axis=0)
    for core in range(CORES):
        for k in range(rows // CORES):
            at = (core * (rows // CORES) + k) * steps
            out_ref[k * CORES + core] = summed[at : at + steps].astype(out_ref.dtype)


SMEM = pl.BlockSpec(memory_space=pltpu.SMEM)
VMEM = pl.BlockSpec(memory_space=pltpu.VMEM)
HBM = pl.BlockSpec(memory_space=pltpu.HBM)


def near(x):
    return pltpu.with_memory_space_constraint(x, pltpu.VMEM)


def far(x):
    return pltpu.with_memory_space_constraint(x, pltpu.HBM)


def body(
    queries,
    new_keys,
    new_values,
    key_blocks,
    value_blocks,
    slot_rows,
    slot_blocks,
    lengths,
    out_weight,
):
    _, steps, width = queries.shape
    slots, block_len, _ = key_blocks.shape
    heads = HQ * steps
    devices = lax.axis_size("inst")
    chips = devices // CORES
    shares = lax.axis_size("tp")
    me = lax.axis_index("inst").astype(jnp.int32).reshape(1)
    core_pairs = [(i, i ^ 1) for i in range(devices)]
    params = pltpu.CompilerParams(vmem_limit_bytes=24 * 1024 * 1024)

    def over_chips(x, order):
        same_core = [[chip * CORES + core for chip in order] for core in range(CORES)]
        return lax.all_to_all(x, "inst", 0, 0, tiled=True, axis_index_groups=same_core)

    other = lax.ppermute(queries, "inst", core_pairs)
    query, fresh, picks, plan = pl.pallas_call(
        functools.partial(plan_kernel, block_len),
        out_shape=[
            pltpu.VMEM((steps, width), jnp.bfloat16),
            pltpu.VMEM((3, heads, HD), jnp.float32),
            pltpu.VMEM((2, HD, width), jnp.bfloat16),
            pltpu.SMEM((4 + 2 * slots,), jnp.int32),
        ],
        in_specs=[SMEM] + [HBM] * 6,
        out_specs=[VMEM] * 3 + [SMEM],
        scratch_shapes=[
            pltpu.SMEM((slots,), jnp.int32),
            pltpu.SMEM((slots,), jnp.int32),
            pltpu.SMEM(lengths.shape, jnp.int32),
            pltpu.VMEM((steps, HD), jnp.bfloat16),
            pltpu.VMEM((steps, HD), jnp.bfloat16),
            pltpu.SemaphoreType.DMA((6,)),
        ],
        compiler_params=params,
        cost_estimate=pl.CostEstimate(flops=1_000_000, bytes_accessed=3_000_000, transcendentals=0),
        name="plan",
    )(me, *map(far, (slot_rows, slot_blocks, lengths, queries, new_keys, new_values)))
    plan = pltpu.with_memory_space_constraint(plan, pltpu.SMEM)
    picks = near(picks)
    spread = pl.pallas_call(
        spread_kernel,
        out_shape=pltpu.VMEM((chips, steps, width), jnp.bfloat16),
        in_specs=[SMEM, VMEM, VMEM],
        out_specs=VMEM,
        compiler_params=params,
        cost_estimate=pl.CostEstimate(
            flops=40_000_000_000, bytes_accessed=60_000_000, transcendentals=0
        ),
        name="spread",
    )(plan, near(query), other)
    asked = over_chips(spread, ASK_ORDER)
    sent_cols = 2 * width + HD
    partial = pl.pallas_call(
        attend_kernel,
        out_shape=pltpu.VMEM((chips, steps, sent_cols), jnp.bfloat16),
        in_specs=[SMEM] + [VMEM] * 5,
        out_specs=VMEM,
        scratch_shapes=[
            pltpu.VMEM((2, heads, HD), jnp.bfloat16),
            pltpu.VMEM((slots, heads, block_len), jnp.float32),
        ],
        compiler_params=params,
        cost_estimate=pl.CostEstimate(
            flops=300_000_000, bytes_accessed=9_000_000, transcendentals=600_000
        ),
        name="attend",
    )(plan, asked, near(query), near(fresh), near(key_blocks), near(value_blocks))
    everyone = over_chips(partial, SEND_ORDER)
    everyone = everyone.reshape(chips * steps, sent_cols)
    share = pl.pallas_call(
        functools.partial(project_kernel, steps, 3 + 2 * slots),
        out_shape=jax.ShapeDtypeStruct(
            (shares, devices * steps // shares, out_weight.shape[1]), jnp.bfloat16
        ),
        in_specs=[SMEM] + [VMEM] * 4,
        out_specs=VMEM,
        compiler_params=params,
        name="project",
    )(plan, picks, everyone, lax.ppermute(everyone, "inst", core_pairs), near(out_weight))
    shared = lax.all_to_all(share, "tp", 0, 0, tiled=True, axis_index_groups=[TP_ORDER])
    return pl.pallas_call(
        add_kernel,
        out_shape=jax.ShapeDtypeStruct(
            (devices // shares, steps, out_weight.shape[1]), jnp.bfloat16
        ),
        in_specs=[VMEM],
        out_specs=VMEM,
        compiler_params=params,
        name="add",
    )(shared)


def solution(mesh):
    in_specs = (
        P("inst", None, "tp"),
        P("inst", None, "tp"),
        P("inst", None, "tp"),
        P("inst", None, "tp"),
        P("inst", None, "tp"),
        P("inst"),
        P("inst"),
        P(),
        P("tp", "inst"),
    )
    out_specs = P("tp", None, "inst")
    return jax.shard_map(body, mesh=mesh, in_specs=in_specs, out_specs=out_specs, check_vma=False)
```

```python
import functools
import math

import jax
import jax.numpy as jnp
from jax import lax
from jax.experimental import pallas as pl
from jax.experimental.pallas import tpu as pltpu
from jax.sharding import PartitionSpec as P

HQ = 8
HD = 128
WIDTH = HQ * HD
NEG = -1e30
FLOOR = -1e29
C = HD ** (-0.5) / math.log(2.0)
PIECES = 3
CORES = 2
UNITS = 2
MXU = 256
ASK_ORDER = [10, 11, 8, 9, 15, 12, 13, 14, 0, 1, 2, 3, 5, 6, 7, 4]
SEND_ORDER = [10, 11, 8, 9, 15, 12, 13, 14, 0, 1, 2, 3, 5, 6, 7, 4]
TP_ORDER = [4, 0, 5, 1, 6, 2, 7, 3]


def longest_row(lengths_ref):
    row, most = jnp.int32(0), lengths_ref[0]
    for r in range(1, lengths_ref.shape[0]):
        here = lengths_ref[r]
        row = jnp.where(here > most, r, row)
        most = jnp.maximum(here, most)
    return row


def pieces_of(x):
    parts = []
    for _ in range(PIECES):
        part = x.astype(jnp.bfloat16).astype(jnp.float32)
        parts.append(part)
        x = x - part
    return parts


def rows_of_heads(q):
    return jnp.concatenate([q[:, h * HD : (h + 1) * HD] for h in range(HQ)], axis=0)


def plan_kernel(
    block_len,
    me_ref,
    rows_hbm,
    blocks_hbm,
    lengths_hbm,
    query_hbm,
    new_key_hbm,
    new_value_hbm,
    query_ref,
    fresh_ref,
    picks_ref,
    plan_ref,
    rows_ref,
    blocks_ref,
    lengths_ref,
    new_key_ref,
    new_value_ref,
    sems,
):
    slots = rows_ref.shape[0]
    steps = query_ref.shape[0]
    heads = HQ * steps
    copies = [
        pltpu.make_async_copy(source, target, sems.at[k])
        for k, (source, target) in enumerate(
            [
                (lengths_hbm, lengths_ref),
                (query_hbm.at[0], query_ref),
                (rows_hbm, rows_ref),
                (blocks_hbm, blocks_ref),
                (new_key_hbm.at[0], new_key_ref),
                (new_value_hbm.at[0], new_value_ref),
            ]
        )
    ]
    for copy in copies:
        copy.start()

    lane = lax.broadcasted_iota(jnp.int32, (HD, WIDTH), 0)
    chosen = lane % HQ == lax.broadcasted_iota(jnp.int32, (HD, WIDTH), 1) // HD
    split = PIECES * HQ
    picks_ref[0] = jnp.where(chosen & (lane < split), 1.0, 0.0).astype(jnp.bfloat16)
    picks_ref[1] = jnp.where(chosen & (lane >= split), 1.0, 0.0).astype(jnp.bfloat16)

    for copy in copies:
        copy.wait()
    me = me_ref[0]
    longest = longest_row(lengths_ref)
    plan_ref[0] = longest
    plan_ref[1] = me
    for at, order in enumerate((ASK_ORDER, SEND_ORDER)):
        place = jnp.int32(0)
        for k, chip in enumerate(order):
            place = jnp.where(longest // CORES == chip, k, place)
        plan_ref[2 + 2 * slots + at] = place
    for s in range(slots):
        row = rows_ref[s]
        in_long = row == longest
        valid = jnp.clip(lengths_ref[row] - blocks_ref[s] * block_len, 0, block_len)
        plan_ref[2 + s] = in_long.astype(jnp.int32)
        plan_ref[2 + slots + s] = jnp.where(in_long | (row == me), valid, 0)

    query = rows_of_heads(query_ref[...].astype(jnp.float32))
    step_of = lax.broadcasted_iota(jnp.int32, (heads, 1), 0) % steps
    fresh = []
    for u in range(steps):
        score = jnp.sum(
            query * new_key_ref[u : u + 1, :].astype(jnp.float32), axis=1, keepdims=True
        )
        fresh.append(jnp.where(step_of >= u, score, NEG))
    top = functools.reduce(jnp.maximum, fresh)
    total = jnp.zeros_like(top)
    acc = jnp.zeros((heads, HD), jnp.float32)
    for u in range(steps):
        weight = jnp.exp2((fresh[u] - top) * C)
        total += weight
        acc += weight.astype(jnp.bfloat16).astype(jnp.float32) * new_value_ref[
            u : u + 1, :
        ].astype(jnp.float32)
    fresh_ref[0] = jnp.broadcast_to(top, (heads, HD))
    fresh_ref[1] = jnp.broadcast_to(total, (heads, HD))
    fresh_ref[2] = acc


def spread_kernel(plan_ref, query_ref, other_ref, spread_ref):
    me = plan_ref[1]
    asked = jnp.where(
        me + 1 - 2 * (me % CORES) == plan_ref[0],
        other_ref[0].astype(jnp.float32),
        query_ref[...].astype(jnp.float32),
    ).astype(jnp.bfloat16)
    spread_ref[...] = jnp.broadcast_to(asked[None], spread_ref.shape)


def attend_kernel(*refs):
    rows = 2 * refs[-2].shape[1]
    pl.run_scoped(
        lambda *sums: attend(*refs, [sums[: len(sums) // UNITS], sums[len(sums) // UNITS :]]),
        *[pltpu.ACC(unit)((rows, MXU), jnp.float32) for unit in range(UNITS) for _ in range(4)],
    )


def attend(
    plan_ref,
    asked_ref,
    query_ref,
    fresh_ref,
    key_ref,
    value_ref,
    out_ref,
    queries,
    scores,
    sums,
):
    slots, block_len, _ = key_ref.shape
    steps = query_ref.shape[0]
    heads = HQ * steps
    longest = plan_ref[0]
    mine = plan_ref[1] == longest
    queries[0] = rows_of_heads(query_ref[...].astype(jnp.float32)).astype(jnp.bfloat16)
    queries[1] = rows_of_heads(asked_ref[plan_ref[2 + 2 * slots]].astype(jnp.float32)).astype(jnp.bfloat16)

    tiles = block_len // MXU
    column = lax.broadcasted_iota(jnp.int32, (heads, MXU), 1)
    high = {}

    def keep(s, tile, product):
        for k in range(2):
            score = product[k * heads : (k + 1) * heads]
            valid = plan_ref[2 + slots + s + k] - tile * MXU
            score = jnp.where(column < valid, score, NEG)
            scores[s + k, :, tile * MXU : (tile + 1) * MXU] = score
            most = functools.reduce(
                jnp.maximum, [score[:, at : at + HD] for at in range(0, MXU, HD)]
            )
            high[s + k] = jnp.maximum(high[s + k], most) if s + k in high else most

    pending = []
    for n, (s, tile) in enumerate((s, t) for s in range(0, slots, 2) for t in range(tiles)):
        if tile == 0:
            first, second = queries[plan_ref[2 + s]], queries[plan_ref[3 + s]]
            none = jnp.zeros_like(first)
            query = jnp.concatenate(
                [
                    jnp.concatenate([first, none], axis=1),
                    jnp.concatenate([none, second], axis=1),
                ],
                axis=0,
            )
        unit, turn = n % UNITS, n // UNITS
        rows = slice(tile * MXU, (tile + 1) * MXU)
        both = jnp.concatenate([key_ref[s, rows], key_ref[s + 1, rows]], axis=1)
        pltpu.matmul_push_rhs(both, turn % 2, unit, transpose=True)
        into = sums[unit][turn % len(sums[unit])]
        pltpu.matmul_acc_lhs(into, query, load_staged_rhs=turn % 2)
        pending.append((s, tile, into))
        if len(pending) > UNITS * (len(sums[unit]) - 1):
            then, at, done = pending.pop(0)
            keep(then, at, pltpu.matmul_pop(done))
    for then, at, done in pending:
        keep(then, at, pltpu.matmul_pop(done))
    tops = [
        jnp.maximum(jnp.max(high[s], axis=1, keepdims=True), FLOOR) for s in range(slots)
    ]

    parts = [(mine, fresh_ref[0][:, :1], fresh_ref[1][:, :1], fresh_ref[2])]

    for s in range(0, slots, 2):
        weights = [jnp.exp2((scores[s + k] - tops[s + k]) * C) for k in range(2)]
        rounded = jnp.concatenate(weights, axis=0).astype(jnp.bfloat16)
        turn = s // 2 % 2
        for tile in range(tiles):
            rows = slice(tile * MXU, (tile + 1) * MXU)
            both = jnp.concatenate([value_ref[s, rows], value_ref[s + 1, rows]], axis=1)
            unit, stage = tile % UNITS, tile // UNITS % 2
            pltpu.matmul_push_rhs(both, stage, unit)
            pltpu.matmul_acc_lhs(sums[unit][turn], rounded[:, rows], load_staged_rhs=stage)
        product = sum(pltpu.matmul_pop(sums[unit][turn]) for unit in range(UNITS))
        for k in range(2):
            acc = product[k * heads : (k + 1) * heads, k * HD : (k + 1) * HD]
            total = jnp.sum(weights[k], axis=1, keepdims=True)
            parts.append((plan_ref[2 + s + k] == 1, tops[s + k], total, acc))

    merged = []
    for wanted in (False, True):
        best = functools.reduce(
            jnp.maximum, [jnp.where(in_long == wanted, top, FLOOR) for in_long, top, _, _ in parts]
        )
        sum_all = jnp.zeros_like(best)
        acc_all = jnp.zeros((heads, HD), jnp.float32)
        for in_long, top, total, acc in parts:
            factor = jnp.where(in_long == wanted, jnp.exp2(jnp.minimum(top - best, 0.0) * C), 0.0)
            sum_all += factor * total
            acc_all += factor * acc
        merged.append((best, sum_all, acc_all))

    _, own_sum, own_acc = merged[0]
    attended = own_acc / jnp.where(own_sum > 0.0, own_sum, 1.0)
    long_top, long_sum, long_acc = merged[1]
    stats = pieces_of(long_top) + pieces_of(long_sum)
    lane = lax.broadcasted_iota(jnp.int32, (steps, HD), 1)
    packed = jnp.zeros((steps, HD), jnp.float32)
    for h in range(HQ):
        rows = slice(h * steps, (h + 1) * steps)
        for k, piece in enumerate(stats):
            packed = jnp.where(lane == k * HQ + h, piece[rows], packed)
    heads_of = lambda x: [x[h * steps : (h + 1) * steps] for h in range(HQ)]
    sent = jnp.concatenate(heads_of(attended) + heads_of(long_acc) + [packed], axis=1)
    out_ref[...] = jnp.broadcast_to(sent.astype(jnp.bfloat16)[None], out_ref.shape)


def project_kernel(steps, place_at, plan_ref, picks_ref, mine_ref, other_ref, weight_ref, out_ref):
    half, _ = mine_ref.shape
    rows = CORES * half
    longest = plan_ref[0]
    first = plan_ref[1] % CORES == 0
    both = lambda cols: jnp.concatenate([mine_ref[:, cols], other_ref[:, cols]], axis=0)
    stats = both(slice(2 * WIDTH, 2 * WIDTH + HD))
    tops = jnp.dot(stats, picks_ref[0], preferred_element_type=jnp.float32)
    sums = jnp.dot(stats, picks_ref[1], preferred_element_type=jnp.float32)
    accs = both(slice(WIDTH, 2 * WIDTH)).astype(jnp.float32)

    pair = 2 * steps
    fold = lambda x: x.reshape(-1, pair, x.shape[-1])
    best = jnp.max(fold(tops), axis=0)
    best = jnp.maximum(best, pltpu.roll(best, steps, 0))
    factor = jnp.exp2((fold(tops) - best[None]) * C)
    total = jnp.sum(factor * fold(sums), axis=0)
    weighted = jnp.sum(factor * fold(accs), axis=0)
    total = total + pltpu.roll(total, steps, 0)
    weighted = weighted + pltpu.roll(weighted, steps, 0)
    merged = weighted / total

    own = mine_ref[:, :WIDTH].astype(jnp.float32)
    other = other_ref[:, :WIDTH].astype(jnp.float32)
    own, other = jnp.where(first, own, other), jnp.where(first, other, own)
    shape = (half // pair, pair, WIDTH)
    place = lax.broadcasted_iota(jnp.int32, shape, 0) * (pair // steps)
    place = place + lax.broadcasted_iota(jnp.int32, shape, 1) // steps
    attended = []
    for core, part in enumerate((own, other)):
        wanted = jnp.where(longest % CORES == core, plan_ref[place_at], -1)
        attended.append(jnp.where(place == wanted, merged[None], fold(part)).reshape(half, WIDTH))
    product = jnp.dot(
        jnp.concatenate(attended, axis=0).astype(jnp.bfloat16),
        weight_ref[...],
        preferred_element_type=jnp.float32,
    )
    shares, each, _ = out_ref.shape
    chips = each // (CORES * steps)
    for k, share in enumerate(TP_ORDER):
        starts = [
            core * half + SEND_ORDER.index(share * chips + chip) * steps
            for core in range(CORES)
            for chip in range(chips)
        ]
        rows = jnp.concatenate([product[at : at + steps] for at in starts], axis=0)
        out_ref[k] = rows.astype(out_ref.dtype)


def add_kernel(shares_ref, out_ref):
    rows, steps, _ = out_ref.shape
    summed = jnp.sum(shares_ref[...].astype(jnp.float32), axis=0)
    for core in range(CORES):
        for k in range(rows // CORES):
            at = (core * (rows // CORES) + k) * steps
            out_ref[k * CORES + core] = summed[at : at + steps].astype(out_ref.dtype)


SMEM = pl.BlockSpec(memory_space=pltpu.SMEM)
VMEM = pl.BlockSpec(memory_space=pltpu.VMEM)
HBM = pl.BlockSpec(memory_space=pltpu.HBM)


def near(x):
    return pltpu.with_memory_space_constraint(x, pltpu.VMEM)


def far(x):
    return pltpu.with_memory_space_constraint(x, pltpu.HBM)


def body(
    queries,
    new_keys,
    new_values,
    key_blocks,
    value_blocks,
    slot_rows,
    slot_blocks,
    lengths,
    out_weight,
):
    _, steps, width = queries.shape
    slots, block_len, _ = key_blocks.shape
    heads = HQ * steps
    devices = lax.axis_size("inst")
    chips = devices // CORES
    shares = lax.axis_size("tp")
    me = lax.axis_index("inst").astype(jnp.int32).reshape(1)
    core_pairs = [(i, i ^ 1) for i in range(devices)]
    params = pltpu.CompilerParams(vmem_limit_bytes=24 * 1024 * 1024)

    def over_chips(x, order):
        same_core = [[chip * CORES + core for chip in order] for core in range(CORES)]
        return lax.all_to_all(x, "inst", 0, 0, tiled=True, axis_index_groups=same_core)

    other = lax.ppermute(queries, "inst", core_pairs)
    query, fresh, picks, plan = pl.pallas_call(
        functools.partial(plan_kernel, block_len),
        out_shape=[
            pltpu.VMEM((steps, width), jnp.bfloat16),
            pltpu.VMEM((3, heads, HD), jnp.float32),
            pltpu.VMEM((2, HD, width), jnp.bfloat16),
            pltpu.SMEM((4 + 2 * slots,), jnp.int32),
        ],
        in_specs=[SMEM] + [HBM] * 6,
        out_specs=[VMEM] * 3 + [SMEM],
        scratch_shapes=[
            pltpu.SMEM((slots,), jnp.int32),
            pltpu.SMEM((slots,), jnp.int32),
            pltpu.SMEM(lengths.shape, jnp.int32),
            pltpu.VMEM((steps, HD), jnp.bfloat16),
            pltpu.VMEM((steps, HD), jnp.bfloat16),
            pltpu.SemaphoreType.DMA((6,)),
        ],
        compiler_params=params,
        cost_estimate=pl.CostEstimate(flops=1_000_000, bytes_accessed=3_000_000, transcendentals=0),
        name="plan",
    )(me, *map(far, (slot_rows, slot_blocks, lengths, queries, new_keys, new_values)))
    plan = pltpu.with_memory_space_constraint(plan, pltpu.SMEM)
    picks = near(picks)
    spread = pl.pallas_call(
        spread_kernel,
        out_shape=pltpu.VMEM((chips, steps, width), jnp.bfloat16),
        in_specs=[SMEM, VMEM, VMEM],
        out_specs=VMEM,
        compiler_params=params,
        cost_estimate=pl.CostEstimate(
            flops=40_000_000_000, bytes_accessed=60_000_000, transcendentals=0
        ),
        name="spread",
    )(plan, near(query), other)
    asked = over_chips(spread, ASK_ORDER)
    sent_cols = 2 * width + HD
    partial = pl.pallas_call(
        attend_kernel,
        out_shape=pltpu.VMEM((chips, steps, sent_cols), jnp.bfloat16),
        in_specs=[SMEM] + [VMEM] * 5,
        out_specs=VMEM,
        scratch_shapes=[
            pltpu.VMEM((2, heads, HD), jnp.bfloat16),
            pltpu.VMEM((slots, heads, block_len), jnp.float32),
        ],
        compiler_params=params,
        cost_estimate=pl.CostEstimate(
            flops=300_000_000, bytes_accessed=9_000_000, transcendentals=600_000
        ),
        name="attend",
    )(plan, asked, near(query), near(fresh), near(key_blocks), near(value_blocks))
    everyone = over_chips(partial, SEND_ORDER)
    everyone = everyone.reshape(chips * steps, sent_cols)
    share = pl.pallas_call(
        functools.partial(project_kernel, steps, 3 + 2 * slots),
        out_shape=jax.ShapeDtypeStruct(
            (shares, devices * steps // shares, out_weight.shape[1]), jnp.bfloat16
        ),
        in_specs=[SMEM] + [VMEM] * 4,
        out_specs=VMEM,
        compiler_params=params,
        name="project",
    )(plan, picks, everyone, lax.ppermute(everyone, "inst", core_pairs), near(out_weight))
    shared = lax.all_to_all(share, "tp", 0, 0, tiled=True, axis_index_groups=[TP_ORDER])
    return pl.pallas_call(
        add_kernel,
        out_shape=jax.ShapeDtypeStruct(
            (devices // shares, steps, out_weight.shape[1]), jnp.bfloat16
        ),
        in_specs=[VMEM],
        out_specs=VMEM,
        compiler_params=params,
        name="add",
    )(shared)


def solution(mesh):
    in_specs = (
        P("inst", None, "tp"),
        P("inst", None, "tp"),
        P("inst", None, "tp"),
        P("inst", None, "tp"),
        P("inst", None, "tp"),
        P("inst"),
        P("inst"),
        P(),
        P("tp", "inst"),
    )
    out_specs = P("tp", None, "inst")
    return jax.shard_map(body, mesh=mesh, in_specs=in_specs, out_specs=out_specs, check_vma=False)
```
